32 devices in a mesh: groups: 2 (over y), seq: 4 (over z), head: 4 (over x, core).
Axes of the slice: x: 2, y: 2, z: 4, core: 2. Of those that a mesh axis runs over, the one named last changes fastest.
Arguments:
- query_rows: bfloat16 [4096, 2048], P(('groups', 'seq', 'head')), parts along dimension 0, may hold values from -6 to 6
- key_rows: bfloat16 [4096, 2048], P(('groups', 'seq', 'head')), parts along dimension 0, may hold values from -6 to 6
- value_rows: bfloat16 [4096, 2048], P(('groups', 'seq', 'head')), parts along dimension 0, may hold values from -24 to 24
- grad_rows: bfloat16 [4096, 2048], P(('groups', 'seq', 'head')), parts along dimension 0, may hold values from -6 to 6
- tile_offsets: int32 [8, 7, 3], P('seq'), may hold values from -1 to 1, as said below
- out_weight: bfloat16 [2048, 2048], P('seq', 'head'), may hold values from -0.125 to 0.125
Outputs:
- projected: bfloat16 [4096, 2048], P(('groups', 'seq', 'head')), parts along dimension 0
- grad_query: bfloat16 [4096, 2048], P(('groups', 'seq'), 'head'), parts along dimension 0
- grad_key: bfloat16 [4096, 2048], P(('groups', 'seq'), 'head'), parts along dimension 0
- grad_value: bfloat16 [4096, 2048], P(('groups', 'seq'), 'head'), parts along dimension 0
The draws below stay inside these ranges and needn't reach their ends.
There are 2 independent parts, one for each index of `groups`. The reference program is written for one: setup_inputs(seed, part) draws one part's arguments, and reference() takes and returns one part's arrays. A program takes and returns all parts, laid end to end along the dimension named above; an argument that names none is the same for every part. Nothing has to cross between parts.
Inputs may be any that keep to these rules, and one draw needn't show every extreme that they name: tile_offsets[c, 0] is (0, 0, 0); the 7 offsets of a tile are distinct, and in each at most one of the row and column entries is nonzero.
All inputs are finite; a program needn't handle non-finite values.
Results may differ from the reference program's by a relative error of at most 0.02.
Values may be sent and summed in bfloat16 or wider, within the bound.
A program may use at most 128 MiB of HBM per device.

```python
import jax
import jax.numpy as jnp
import numpy as np
from jax import lax

HEADS = 16
HEAD_DIM = 128
D = 2048
TILE = 256
TT = 2
TH = 2
WIN = 7
TW = 2
NTILES = 8
TOKENS = 2048
N_HEAD = 4


cross_offsets = np.array([[step_t, step_h, step_w] for step_t in (-1, 0, 1) for step_h, step_w in ((0, 0), (1, 0), (-1, 0), (0, 1), (0, -1)) if (step_t, step_h, step_w) != (0, 0, 0)], dtype=np.int32)


def draw_query_rows(key, part):
    key = jax.random.fold_in(key, 11)
    field = jnp.clip(1.2 * jax.random.normal(key, (TOKENS, D), jnp.float32), -6.0, 6.0)
    return field.astype(jnp.bfloat16)


def draw_key_rows(key, part):
    key = jax.random.fold_in(key, 23)
    field = jnp.clip(1.2 * jax.random.normal(key, (TOKENS, D), jnp.float32), -6.0, 6.0)
    return field.astype(jnp.bfloat16)


def draw_tile_offsets(key, part):
    key = jax.random.fold_in(key, 37)
    subkeys = jax.random.split(key, NTILES)
    ranking = jax.vmap(lambda single: jax.random.permutation(single, 14))(subkeys)
    chosen = jnp.asarray(cross_offsets)[ranking[:, :WIN - 1]]
    centre = jnp.zeros((NTILES, 1, 3), jnp.int32)
    return jnp.concatenate([centre, chosen], axis=1).astype(jnp.int32)


def shard_levels(stream_key, extent, pieces, low, high):
    factor_of, own = 1.0, jax.random.fold_in(stream_key, 6)
    for axis_at, shards_of in pieces:
        draws = jnp.exp(jax.random.uniform(jax.random.fold_in(own, axis_at), (shards_of,), jnp.float32, low / len(pieces), high / len(pieces)))
        factor_of = factor_of * jnp.repeat(draws, extent[axis_at] // shards_of).reshape([-1 if axis == axis_at else 1 for axis in range(len(extent))])
    return factor_of


def bell_draw(key, dims, deviation, bound, pieces=(), held_as=jnp.bfloat16):
    values = deviation * jax.random.normal(key, dims, jnp.float32)
    if pieces:
        values = values * shard_levels(key, dims, pieces, -0.22, 0.18)
    return jnp.clip(values, -bound, bound).astype(held_as)


def setup_inputs(seed: int = 0, part: int = 0) -> dict:
    key_of = jax.random.split(jax.random.key(seed), 7)
    part_splits = jax.random.split(jax.random.fold_in(key_of[6], part), 7)
    return {
        "query_rows": draw_query_rows(jax.random.fold_in(jax.random.fold_in(key_of[6], part), 71), part),
        "key_rows": draw_key_rows(jax.random.fold_in(jax.random.fold_in(key_of[6], part), 71), part),
        "value_rows": bell_draw(part_splits[2], (TOKENS, D), 4.0, 24.0, ((0, 16),)),
        "grad_rows": bell_draw(part_splits[3], (TOKENS, D), 1.0, 6.0, ((0, 16),)),
        "tile_offsets": draw_tile_offsets(jax.random.fold_in(key_of[6], 71), part),
        "out_weight": bell_draw(key_of[5], (D, D), D ** -0.5, 0.125, ((0, 4), (1, 4))),
    }


def route_of(row_step, col_step):
    return jnp.where(row_step == 1, 1, jnp.where(row_step == -1, 2, jnp.where(col_step == 1, 3, jnp.where(col_step == -1, 4, 0)))).astype(jnp.int32)


def tile_layout(tile_offsets):
    tile_ids = jnp.arange(NTILES, dtype=jnp.int32)
    time_tile = tile_ids % TT
    row_tile = (tile_ids // TT) % TH
    col_tile = tile_ids // (TT * TH)
    key_time = time_tile[:, None] + tile_offsets[:, :, 0]
    key_row = row_tile[:, None] + tile_offsets[:, :, 1]
    key_col = col_tile[:, None] + tile_offsets[:, :, 2]
    inside = (key_time >= 0) & (key_time < TT) & (key_row >= 0) & (key_row < TH) & (key_col >= 0) & (key_col < TW)
    target = (jnp.clip(key_col, 0, TW - 1) * TH + jnp.clip(key_row, 0, TH - 1)) * TT + jnp.clip(key_time, 0, TT - 1)
    routes = route_of(tile_offsets[:, :, 1], tile_offsets[:, :, 2])
    return inside, target.astype(jnp.int32), routes


def reference(query_rows, key_rows, value_rows, grad_rows, tile_offsets, out_weight):
    inside, target, routes = tile_layout(tile_offsets)
    score_scale = HEAD_DIM ** -0.5
    segment_ids = (target * 5 + routes).reshape(-1)

    def settle(terms):
        flat_terms = terms.reshape(NTILES * WIN, TILE, HEAD_DIM)
        grouped = jax.ops.segment_sum(flat_terms, segment_ids, num_segments=NTILES * 5)
        grouped = grouped.reshape(NTILES, 5, TILE, HEAD_DIM)
        remote = lax.optimization_barrier(grouped[:, 1:].astype(jnp.bfloat16)).astype(jnp.float32)
        return (grouped[:, 0] + jnp.sum(remote, axis=1)).astype(jnp.bfloat16)

    def one_head(operands):
        head_query, head_key, head_value, head_grad = operands
        query_f = head_query.astype(jnp.float32)
        grad_f = head_grad.astype(jnp.float32)
        near_keys = head_key[target].astype(jnp.float32)
        near_values = head_value[target].astype(jnp.float32)
        scores = jnp.einsum("cid,cwjd->ciwj", query_f, near_keys) * score_scale
        scores = jnp.where(inside[:, None, :, None], scores, -jnp.inf)
        row_max = jnp.max(scores, axis=(2, 3), keepdims=True)
        exp_scores = jnp.exp(scores - row_max)
        row_sum = jnp.sum(exp_scores, axis=(2, 3), keepdims=True)
        weights = (exp_scores / row_sum).astype(jnp.bfloat16)
        weights_f = weights.astype(jnp.float32)
        attended = jnp.einsum("ciwj,cwjd->cid", weights_f, near_values).astype(jnp.bfloat16)
        row_dot = jnp.sum(grad_f * attended.astype(jnp.float32), axis=-1)
        grad_weights = jnp.einsum("cid,cwjd->ciwj", grad_f, near_values)
        grad_scores = (weights_f * (grad_weights - row_dot[:, :, None, None])).astype(jnp.bfloat16)
        grad_scores_f = grad_scores.astype(jnp.float32)
        query_grad = (score_scale * jnp.einsum("ciwj,cwjd->cid", grad_scores_f, near_keys)).astype(jnp.bfloat16)
        key_terms = score_scale * jnp.einsum("ciwj,cid->cwjd", grad_scores_f, query_f)
        value_terms = jnp.einsum("ciwj,cid->cwjd", weights_f, grad_f)
        return attended, query_grad, settle(key_terms), settle(value_terms)

    def by_head(matrix):
        return matrix.reshape(NTILES, TILE, HEADS, HEAD_DIM).transpose(2, 0, 1, 3)

    def by_token(stacked):
        return stacked.transpose(1, 2, 0, 3).reshape(TOKENS, HEADS * HEAD_DIM)

    outputs = lax.map(one_head, (by_head(query_rows), by_head(key_rows), by_head(value_rows), by_head(grad_rows)))
    attended, grad_query, grad_key, grad_value = [by_token(item) for item in outputs]
    group_width = HEADS // N_HEAD * HEAD_DIM
    projected = jnp.zeros((TOKENS, HEADS * HEAD_DIM), jnp.float32)
    for group_id in range(N_HEAD):
        group_cols = attended[:, group_id * group_width:(group_id + 1) * group_width]
        group_rows = out_weight[:, group_id * group_width:(group_id + 1) * group_width]
        group_term = jnp.dot(group_cols, group_rows.T, preferred_element_type=jnp.float32)
        projected = projected + lax.optimization_barrier(group_term.astype(jnp.bfloat16)).astype(jnp.float32)
    return projected.astype(jnp.bfloat16), grad_query, grad_key, grad_value
```

```python
import functools

import jax
import jax.numpy as jnp
from jax import lax
from jax.experimental import pallas as pl
from jax.experimental.pallas import tpu as pltpu
from jax.sharding import PartitionSpec as P

HEADS = 16
HEAD_DIM = 128
TILE = 256
TT = 2
TH = 2
SCALE = HEAD_DIM ** (-0.5)
DEAD = -1e30


def dot(a, b, ca, cb):
    return lax.dot_general(a, b, (((ca,), (cb,)), ((), ())), preferred_element_type=jnp.float32)


def live_bias(tile_offsets, position, steps):
    row_tile, col_tile = position % TH, position // TH
    query_time = jnp.arange(TT, dtype=jnp.int32)
    rows = []
    for step_r, step_c, there in steps(row_tile, col_tile):
        for key_time in range(TT):
            hit = (
                (tile_offsets[:, :, 0] == key_time - query_time[:, None])
                & (tile_offsets[:, :, 1] == step_r)
                & (tile_offsets[:, :, 2] == step_c)
            )
            rows.append(jnp.any(hit, axis=1) & there)
    live = jnp.stack(rows)
    return jnp.repeat(jnp.where(live, 0.0, DEAD).astype(jnp.float32), TILE, axis=1)


def one_head(q, g, key_of, value_of, bias_ref, blocks, s_scr, w_scr, put_key, put_value):
    top = None
    for b in range(blocks):
        s = dot(key_of(b), q, 1, 1) * SCALE + bias_ref[b : b + 1, :]
        s_scr[b] = s
        high = jnp.max(s, axis=0, keepdims=True)
        top = high if top is None else jnp.maximum(top, high)
    total = None
    for b in range(blocks):
        p = jnp.exp(s_scr[b] - top)
        s_scr[b] = p
        part = jnp.sum(p, axis=0, keepdims=True)
        total = part if total is None else total + part
    share = 1.0 / total
    att = None
    for b in range(blocks):
        w = (s_scr[b] * share).astype(jnp.bfloat16)
        w_scr[b] = w
        part = dot(value_of(b), w, 0, 0)
        att = part if att is None else att + part
        put_value(b, dot(w, g, 1, 0))
    att = att.astype(jnp.bfloat16).astype(jnp.float32)
    row_dot = jnp.sum(att * g.astype(jnp.float32).T, axis=0, keepdims=True)
    dq = None
    for b in range(blocks):
        dw = dot(value_of(b), g, 1, 1)
        ds = (w_scr[b].astype(jnp.float32) * (dw - row_dot)).astype(jnp.bfloat16)
        part = dot(key_of(b), ds, 0, 0)
        dq = part if dq is None else dq + part
        put_key(b, dot(ds, q, 1, 0) * SCALE)
    return att.T.astype(jnp.bfloat16), (dq * SCALE).T.astype(jnp.bfloat16)


def attend_kernel(routes, *refs):
    bias_ref, q_ref, g_ref = refs[:3]
    k_refs, v_refs = refs[3 : 3 + routes], refs[3 + routes : 3 + 2 * routes]
    outs = refs[3 + 2 * routes :]
    att_ref, dq_ref = outs[:2]
    dk_refs, dv_refs = outs[2 : 2 + routes], outs[2 + routes : 2 + 2 * routes]
    s_scr, w_scr = outs[2 + 2 * routes :]

    def rows(b):
        return slice((b % TT) * TILE, (b % TT + 1) * TILE)

    def put(refs_of):
        def store(b, value):
            refs_of[b // TT][rows(b), :] = value.astype(refs_of[b // TT].dtype)

        return store

    att_ref[...], dq_ref[...] = one_head(
        q_ref[...],
        g_ref[...],
        lambda b: k_refs[b // TT][rows(b), :],
        lambda b: v_refs[b // TT][rows(b), :],
        bias_ref,
        routes * TT,
        s_scr,
        w_scr,
        put(dk_refs),
        put(dv_refs),
    )


def attend(bias, query, grad, keys, values):
    routes = len(keys)
    slab, width = query.shape
    block = pl.BlockSpec((slab, HEAD_DIM), lambda h: (0, h))
    sums = [jax.ShapeDtypeStruct((slab, width), jnp.float32 if r == 0 else jnp.bfloat16) for r in range(routes)]
    like = jax.ShapeDtypeStruct((slab, width), jnp.bfloat16)
    outs = pl.pallas_call(
        functools.partial(attend_kernel, routes),
        grid=(width // HEAD_DIM,),
        in_specs=[pl.BlockSpec(bias.shape, lambda h: (0, 0))] + [block] * (2 + 2 * routes),
        out_specs=[block] * (2 + 2 * routes),
        out_shape=[like, like] + sums + sums,
        scratch_shapes=[
            pltpu.VMEM((routes * TT, TILE, slab), jnp.float32),
            pltpu.VMEM((routes * TT, TILE, slab), jnp.bfloat16),
        ],
        compiler_params=pltpu.CompilerParams(vmem_limit_bytes=48 * 2**20),
        name="attend",
    )(bias, query, grad, *keys, *values)
    return outs[0], outs[1], outs[2 : 2 + routes], outs[2 + routes :]


def routes_of(col_count):
    seq = col_count * TH
    moves = [[(s, s ^ 1) for s in range(seq)]]
    if col_count == 2:
        moves.append([(s, s ^ TH) for s in range(seq)])
    else:
        moves.append([(s, s + TH) for s in range(seq - TH)])
        moves.append([(s, s - TH) for s in range(TH, seq)])

    def steps(row_tile, col_tile):
        found = [(0, 0, True), (1 - 2 * row_tile, 0, True)]
        if col_count == 2:
            found.append((0, 1 - 2 * col_tile, True))
        else:
            found += [(0, -1, col_tile > 0), (0, 1, col_tile < col_count - 1)]
        return found

    return moves, steps


def body(query_rows, key_rows, value_rows, grad_rows, tile_offsets, out_weight):
    seq = lax.axis_size("seq")
    moves, steps = routes_of(seq // TH)
    bias = live_bias(tile_offsets, lax.axis_index("seq"), steps)
    weight = lax.all_gather(out_weight, "seq", axis=0, tiled=True)
    key_h, value_h, query_h, grad_h = (
        lax.all_to_all(rows, "head", split_axis=1, concat_axis=0, tiled=True)
        for rows in (key_rows, value_rows, query_rows, grad_rows)
    )
    keys = [key_h] + [lax.ppermute(key_h, "seq", move) for move in moves]
    values = [value_h] + [lax.ppermute(value_h, "seq", move) for move in moves]
    att, dq, dk, dv = attend(bias, query_h, grad_h, keys, values)
    projected = lax.psum_scatter(
        dot(att, weight, 1, 1).astype(jnp.bfloat16), "head", scatter_dimension=0, tiled=True
    )

    def settle(terms):
        total = terms[0]
        for term, move in zip(terms[1:], moves):
            back = [(t, s) for s, t in move]
            total = total + lax.ppermute(term, "seq", back).astype(jnp.float32)
        return total.astype(jnp.bfloat16)

    return projected, dq, settle(dk), settle(dv)


def solution(mesh):
    return jax.shard_map(
        body,
        mesh=mesh,
        in_specs=(
            P(("groups", "seq", "head"), None),
            P(("groups", "seq", "head"), None),
            P(("groups", "seq", "head"), None),
            P(("groups", "seq", "head"), None),
            P("seq", None, None),
            P("seq", "head"),
        ),
        out_specs=(
            P(("groups", "seq", "head"), None),
            P(("groups", "seq"), "head"),
            P(("groups", "seq"), "head"),
            P(("groups", "seq"), "head"),
        ),
        check_vma=False,
    )
```

```python
import functools

import jax
import jax.numpy as jnp
from jax import lax
from jax.experimental import pallas as pl
from jax.experimental.pallas import tpu as pltpu
from jax.sharding import PartitionSpec as P

HEADS = 16
HEAD_DIM = 128
TILE = 256
TT = 2
TH = 2
SCALE = HEAD_DIM ** (-0.5)
DEAD = -1e30


def dot(a, b, ca, cb):
    return lax.dot_general(a, b, (((ca,), (cb,)), ((), ())), preferred_element_type=jnp.float32)


def live_bias(tile_offsets, position, steps):
    row_tile, col_tile = position % TH, position // TH
    query_time = jnp.arange(TT, dtype=jnp.int32)
    rows = []
    for step_r, step_c, there in steps(row_tile, col_tile):
        for key_time in range(TT):
            hit = (
                (tile_offsets[:, :, 0] == key_time - query_time[:, None])
                & (tile_offsets[:, :, 1] == step_r)
                & (tile_offsets[:, :, 2] == step_c)
            )
            rows.append(jnp.any(hit, axis=1) & there)
    live = jnp.stack(rows)
    return jnp.repeat(jnp.where(live, 0.0, DEAD).astype(jnp.float32), TILE, axis=1)


def one_head(q, g, key_of, value_of, bias_ref, blocks, s_scr, w_scr, put_key, put_value):
    top = None
    for b in range(blocks):
        s = dot(key_of(b), q, 1, 1) * SCALE + bias_ref[b : b + 1, :]
        s_scr[b] = s
        high = jnp.max(s, axis=0, keepdims=True)
        top = high if top is None else jnp.maximum(top, high)
    total = None
    for b in range(blocks):
        p = jnp.exp(s_scr[b] - top)
        s_scr[b] = p
        part = jnp.sum(p, axis=0, keepdims=True)
        total = part if total is None else total + part
    share = 1.0 / total
    att = None
    for b in range(blocks):
        w = (s_scr[b] * share).astype(jnp.bfloat16)
        w_scr[b] = w
        part = dot(value_of(b), w, 0, 0)
        att = part if att is None else att + part
        put_value(b, dot(w, g, 1, 0))
    att = att.astype(jnp.bfloat16).astype(jnp.float32)
    row_dot = jnp.sum(att * g.astype(jnp.float32).T, axis=0, keepdims=True)
    dq = None
    for b in range(blocks):
        dw = dot(value_of(b), g, 1, 1)
        ds = (w_scr[b].astype(jnp.float32) * (dw - row_dot)).astype(jnp.bfloat16)
        part = dot(key_of(b), ds, 0, 0)
        dq = part if dq is None else dq + part
        put_key(b, dot(ds, q, 1, 0) * SCALE)
    return att.T.astype(jnp.bfloat16), (dq * SCALE).T.astype(jnp.bfloat16)


def attend_kernel(routes, *refs):
    bias_ref, q_ref, g_ref = refs[:3]
    k_refs, v_refs = refs[3 : 3 + routes], refs[3 + routes : 3 + 2 * routes]
    outs = refs[3 + 2 * routes :]
    att_ref, dq_ref = outs[:2]
    dk_refs, dv_refs = outs[2 : 2 + routes], outs[2 + routes : 2 + 2 * routes]
    s_scr, w_scr = outs[2 + 2 * routes :]

    def rows(b):
        return slice((b % TT) * TILE, (b % TT + 1) * TILE)

    def put(refs_of):
        def store(b, value):
            refs_of[b // TT][rows(b), :] = value.astype(refs_of[b // TT].dtype)

        return store

    att_ref[...], dq_ref[...] = one_head(
        q_ref[...],
        g_ref[...],
        lambda b: k_refs[b // TT][rows(b), :],
        lambda b: v_refs[b // TT][rows(b), :],
        bias_ref,
        routes * TT,
        s_scr,
        w_scr,
        put(dk_refs),
        put(dv_refs),
    )


def attend(bias, query, grad, keys, values):
    routes = len(keys)
    slab, width = query.shape
    block = pl.BlockSpec((slab, HEAD_DIM), lambda h: (0, h))
    sums = [jax.ShapeDtypeStruct((slab, width), jnp.float32 if r == 0 else jnp.bfloat16) for r in range(routes)]
    like = jax.ShapeDtypeStruct((slab, width), jnp.bfloat16)
    outs = pl.pallas_call(
        functools.partial(attend_kernel, routes),
        grid=(width // HEAD_DIM,),
        in_specs=[pl.BlockSpec(bias.shape, lambda h: (0, 0))] + [block] * (2 + 2 * routes),
        out_specs=[block] * (2 + 2 * routes),
        out_shape=[like, like] + sums + sums,
        scratch_shapes=[
            pltpu.VMEM((routes * TT, TILE, slab), jnp.float32),
            pltpu.VMEM((routes * TT, TILE, slab), jnp.bfloat16),
        ],
        compiler_params=pltpu.CompilerParams(vmem_limit_bytes=48 * 2**20),
        name="attend",
    )(bias, query, grad, *keys, *values)
    return outs[0], outs[1], outs[2 : 2 + routes], outs[2 + routes :]


def routes_of(col_count):
    seq = col_count * TH
    moves = [[(s, s ^ 1) for s in range(seq)]]
    if col_count == 2:
        moves.append([(s, s ^ TH) for s in range(seq)])
    else:
        moves.append([(s, s + TH) for s in range(seq - TH)])
        moves.append([(s, s - TH) for s in range(TH, seq)])

    def steps(row_tile, col_tile):
        found = [(0, 0, True), (1 - 2 * row_tile, 0, True)]
        if col_count == 2:
            found.append((0, 1 - 2 * col_tile, True))
        else:
            found += [(0, -1, col_tile > 0), (0, 1, col_tile < col_count - 1)]
        return found

    return moves, steps


MESH = pl.DeviceIdType.MESH


def whole_kernel(groups, seq, head, *refs):
    bias_ref, k_in, v_in, q_in, g_in, w_in = refs[:6]
    proj_ref, dq_ref, dk_ref, dv_ref = refs[6:10]
    mine, near, d_self, d_out, d_in, att, weight, p_out, p_in, p_self, s_scr, w_scr = refs[10:22]
    (x_send, x_recv, x_own, n_send, n_recv, d_send, d_recv, z_send, z_recv, y_send, y_recv, w_own, p_send, p_recv) = refs[22:]
    inputs = (k_in, v_in, q_in, g_in)
    heads, slab = mine.shape[1], mine.shape[2]
    rows = k_in.shape[0]
    half = weight.shape[2]
    width = heads * HEAD_DIM
    me_g, me_s, me_h = lax.axis_index("groups"), lax.axis_index("seq"), lax.axis_index("head")
    beside = (me_s + 1 - 2 * lax.rem(me_s, TH), lax.rem(me_s + TH, seq))

    def at(g=None, s=None, h=None):
        return (me_g if g is None else g, me_s if s is None else s, me_h if h is None else h)

    def after(i):
        return lax.rem(me_h + i, head)

    def before(i):
        return lax.rem(me_h + head - i, head)

    def remote(src, dst, send, recv, device):
        return pltpu.make_async_remote_copy(
            src_ref=src, dst_ref=dst, send_sem=send, recv_sem=recv, device_id=device, device_id_type=MESH
        )

    def columns(owner, h):
        return pl.ds(pl.multiple_of(owner * width + h * HEAD_DIM, HEAD_DIM), HEAD_DIM)

    def row_block(owner):
        return pl.ds(pl.multiple_of(owner * rows, rows), rows)

    def head_move(a, h, i, owner):
        return remote(
            inputs[a].at[:, columns(after(i), h)],
            mine.at[a, h, row_block(owner), :],
            x_send.at[a, h, i - 1],
            x_recv.at[a, h, i - 1],
            at(h=after(i)),
        )

    def head_own(a, h):
        return pltpu.make_async_copy(
            inputs[a].at[:, columns(me_h, h)], mine.at[a, h, row_block(me_h), :], x_own.at[a, h]
        )

    def near_move(j, a, h):
        return remote(mine.at[a, h], near.at[j, a, h], n_send.at[j, a, h], n_recv.at[j, a, h], at(s=beside[j]))

    def grad_move(j, a, h):
        return remote(d_out.at[j, a, h], d_in.at[j, a, h], d_send.at[j, a, h], d_recv.at[j, a, h], at(s=beside[j]))

    def weight_z(i, owner):
        return remote(
            w_in.at[pl.ds(pl.multiple_of(me_g * half, half), half), :],
            weight.at[owner, me_g],
            z_send.at[i - 1],
            z_recv.at[i - 1],
            at(s=lax.rem(me_s + i, seq)),
        )

    def weight_y(i, part):
        owner = lax.rem(me_s + seq - i, seq)
        return remote(
            weight.at[owner, me_g], weight.at[owner, part], y_send.at[i - 1], y_recv.at[i - 1], at(g=1 - me_g)
        )

    def weight_own(part):
        return pltpu.make_async_copy(
            w_in.at[pl.ds(part * half, half), :], weight.at[me_s, part], w_own.at[part]
        )

    def term_move(i):
        return remote(p_out.at[i - 1], p_in.at[i - 1], p_send.at[i - 1], p_recv.at[i - 1], at(h=after(i)))

    barrier = pltpu.get_barrier_semaphore()
    peers = [at(h=after(i)) for i in range(1, head)]
    peers += [at(s=lax.rem(me_s + i, seq)) for i in range(1, seq)] + [at(g=1 - me_g)]
    for peer in peers:
        pl.semaphore_signal(barrier, inc=1, device_id=peer, device_id_type=MESH)
    pl.semaphore_wait(barrier, len(peers))

    def send_inputs(pair):
        def step(h, carry):
            for i in range(1, head):
                for a in pair:
                    head_move(a, h, i, me_h).start()
            for a in pair:
                head_own(a, h).start()
            return carry

        lax.fori_loop(0, heads, step, 0)

    def take_inputs(a, h):
        for i in range(1, head):
            head_move(a, h, i, before(i)).wait_recv()
        head_own(a, h).wait()

    send_inputs((0, 1))
    for i in range(1, seq):
        weight_z(i, me_s).start()
    send_inputs((2, 3))
    for part in range(2):
        weight_own(part).start()

    def pass_on(h, carry):
        for a in range(2):
            take_inputs(a, h)
            for j in (1, 0):
                near_move(j, a, h).start()
        return carry

    lax.fori_loop(0, heads, pass_on, 0)
    for i in range(1, seq):
        weight_z(i, lax.rem(me_s + seq - i, seq)).wait_recv()
        weight_y(i, me_g).start()

    def work(h, carry):
        take_inputs(2, h)
        take_inputs(3, h)
        for j in range(2):
            for a in range(2):
                near_move(j, a, h).wait_recv()

        def tile(b):
            return slice((b % TT) * TILE, (b % TT + 1) * TILE)

        def read(a):
            def of(b):
                r = b // TT
                return mine[a, h, tile(b), :] if r == 0 else near[r - 1, a, h, tile(b), :]

            return of

        def put(a):
            def store(b, value):
                r = b // TT
                if r == 0:
                    d_self[a, h, tile(b), :] = value
                else:
                    d_out[r - 1, a, h, tile(b), :] = value.astype(jnp.bfloat16)

            return store

        attended, dq = one_head(
            mine[2, h], mine[3, h], read(0), read(1), bias_ref, 3 * TT, s_scr, w_scr, put(0), put(1)
        )
        att[:, columns(0, h)] = attended
        dq_ref[:, columns(0, h)] = dq
        for a in range(2):
            for j in (1, 0):
                grad_move(j, a, h).start()
        return carry

    lax.fori_loop(0, heads, work, 0)

    for part in range(2):
        weight_own(part).wait()
    for i in range(1, seq):
        weight_y(i, 1 - me_g).wait_recv()

    def project(owner, store):
        lines = att[row_block(owner), :]
        for s in range(seq):
            for part in range(2):
                start = (s * 2 + part) * half
                store(slice(start, start + half), dot(lines, weight[s, part], 1, 1))

    for i in range(1, head):

        def to_send(cols, value, i=i):
            p_out[i - 1, :, cols] = value.astype(jnp.bfloat16)

        project(after(i), to_send)
        term_move(i).start()

    def to_keep(cols, value):
        p_self[:, cols] = value

    project(me_h, to_keep)

    def settle(h, carry):
        for a, out in ((1, dv_ref), (0, dk_ref)):
            total = d_self[a, h]
            for j in range(2):
                grad_move(j, a, h).wait_recv()
                total = total + d_in[j, a, h].astype(jnp.float32)
            out[:, columns(0, h)] = total.astype(jnp.bfloat16)
        return carry

    lax.fori_loop(0, heads, settle, 0)
    for i in range(1, head):
        term_move(i).wait_recv()
    total = p_self[...]
    for i in range(1, head):
        total = total + p_in[i - 1].astype(jnp.float32)
    proj_ref[...] = total.astype(jnp.bfloat16)

    def drain(h, carry):
        for a in range(4):
            for i in range(1, head):
                head_move(a, h, i, me_h).wait_send()
        for a in range(2):
            for j in range(2):
                near_move(j, a, h).wait_send()
                grad_move(j, a, h).wait_send()
        return carry

    lax.fori_loop(0, heads, drain, 0)
    for i in range(1, seq):
        weight_z(i, me_s).wait_send()
        weight_y(i, me_g).wait_send()
    for i in range(1, head):
        term_move(i).wait_send()


def whole(bias, key_rows, value_rows, query_rows, grad_rows, out_weight):
    groups, seq, head = (lax.axis_size(name) for name in ("groups", "seq", "head"))
    rows, features = key_rows.shape
    slab, width = rows * head, features // head
    heads = width // HEAD_DIM
    half = out_weight.shape[0] // 2
    b16, f32, dma = jnp.bfloat16, jnp.float32, pltpu.SemaphoreType.DMA
    vmem = pl.BlockSpec(memory_space=pltpu.VMEM)
    grads = jax.ShapeDtypeStruct((slab, width), b16)
    return pl.pallas_call(
        functools.partial(whole_kernel, groups, seq, head),
        in_specs=[vmem] + [pl.BlockSpec(memory_space=pl.ANY)] * 5,
        out_specs=[vmem] * 4,
        out_shape=[jax.ShapeDtypeStruct((rows, features), b16), grads, grads, grads],
        scratch_shapes=[
            pltpu.VMEM((4, heads, slab, HEAD_DIM), b16),
            pltpu.VMEM((2, 2, heads, slab, HEAD_DIM), b16),
            pltpu.VMEM((2, heads, slab, HEAD_DIM), f32),
            pltpu.VMEM((2, 2, heads, slab, HEAD_DIM), b16),
            pltpu.VMEM((2, 2, heads, slab, HEAD_DIM), b16),
            pltpu.VMEM((slab, width), b16),
            pltpu.VMEM((seq, 2, half, width), b16),
            pltpu.VMEM((head - 1, rows, features), b16),
            pltpu.VMEM((head - 1, rows, features), b16),
            pltpu.VMEM((rows, features), f32),
            pltpu.VMEM((3 * TT, TILE, slab), f32),
            pltpu.VMEM((3 * TT, TILE, slab), b16),
            dma((4, heads, head - 1)),
            dma((4, heads, head - 1)),
            dma((4, heads)),
            dma((2, 2, heads)),
            dma((2, 2, heads)),
            dma((2, 2, heads)),
            dma((2, 2, heads)),
            dma((seq - 1,)),
            dma((seq - 1,)),
            dma((seq - 1,)),
            dma((seq - 1,)),
            dma((2,)),
            dma((head - 1,)),
            dma((head - 1,)),
        ],
        compiler_params=pltpu.CompilerParams(
            collective_id=0, has_side_effects=True, vmem_limit_bytes=56 * 2**20
        ),
        name="whole",
    )(bias, key_rows, value_rows, query_rows, grad_rows, out_weight)


def body(query_rows, key_rows, value_rows, grad_rows, tile_offsets, out_weight):
    seq = lax.axis_size("seq")
    moves, steps = routes_of(seq // TH)
    bias = live_bias(tile_offsets, lax.axis_index("seq"), steps)
    if seq == 2 * TH and lax.axis_size("groups") == 2:
        return tuple(whole(bias, key_rows, value_rows, query_rows, grad_rows, out_weight))
    weight = lax.all_gather(out_weight, "seq", axis=0, tiled=True)
    key_h, value_h, query_h, grad_h = (
        lax.all_to_all(rows, "head", split_axis=1, concat_axis=0, tiled=True)
        for rows in (key_rows, value_rows, query_rows, grad_rows)
    )
    keys = [key_h] + [lax.ppermute(key_h, "seq", move) for move in moves]
    values = [value_h] + [lax.ppermute(value_h, "seq", move) for move in moves]
    att, dq, dk, dv = attend(bias, query_h, grad_h, keys, values)
    projected = lax.psum_scatter(
        dot(att, weight, 1, 1).astype(jnp.bfloat16), "head", scatter_dimension=0, tiled=True
    )

    def settle(terms):
        total = terms[0]
        for term, move in zip(terms[1:], moves):
            back = [(t, s) for s, t in move]
            total = total + lax.ppermute(term, "seq", back).astype(jnp.float32)
        return total.astype(jnp.bfloat16)

    return projected, dq, settle(dk), settle(dv)


def solution(mesh):
    return jax.shard_map(
        body,
        mesh=mesh,
        in_specs=(
            P(("groups", "seq", "head"), None),
            P(("groups", "seq", "head"), None),
            P(("groups", "seq", "head"), None),
            P(("groups", "seq", "head"), None),
            P("seq", None, None),
            P("seq", "head"),
        ),
        out_specs=(
            P(("groups", "seq", "head"), None),
            P(("groups", "seq"), "head"),
            P(("groups", "seq"), "head"),
            P(("groups", "seq"), "head"),
        ),
        check_vma=False,
    )
```

```python
import functools

import jax
import jax.numpy as jnp
from jax import lax
from jax.experimental import pallas as pl
from jax.experimental.pallas import tpu as pltpu
from jax.sharding import PartitionSpec as P

HEADS = 16
HEAD_DIM = 128
TILE = 256
TT = 2
TH = 2
SCALE = HEAD_DIM ** (-0.5)
DEAD = -1e30


def dot(a, b, ca, cb):
    return lax.dot_general(a, b, (((ca,), (cb,)), ((), ())), preferred_element_type=jnp.float32)


def live_bias(tile_offsets, position, steps):
    row_tile, col_tile = position % TH, position // TH
    query_time = jnp.arange(TT, dtype=jnp.int32)
    rows = []
    for step_r, step_c, there in steps(row_tile, col_tile):
        for key_time in range(TT):
            hit = (
                (tile_offsets[:, :, 0] == key_time - query_time[:, None])
                & (tile_offsets[:, :, 1] == step_r)
                & (tile_offsets[:, :, 2] == step_c)
            )
            rows.append(jnp.any(hit, axis=1) & there)
    live = jnp.stack(rows)
    return jnp.repeat(jnp.where(live, 0.0, DEAD).astype(jnp.float32), TILE, axis=1)


def one_head(q, g, key_of, value_of, bias_ref, blocks, s_scr, w_scr, put_key, put_value):
    top = None
    for b in range(blocks):
        s = dot(key_of(b), q, 1, 1) * SCALE + bias_ref[b : b + 1, :]
        s_scr[b] = s
        high = jnp.max(s, axis=0, keepdims=True)
        top = high if top is None else jnp.maximum(top, high)
    total = None
    for b in range(blocks):
        p = jnp.exp(s_scr[b] - top)
        s_scr[b] = p
        part = jnp.sum(p, axis=0, keepdims=True)
        total = part if total is None else total + part
    share = 1.0 / total
    att = None
    for b in range(blocks):
        w = (s_scr[b] * share).astype(jnp.bfloat16)
        w_scr[b] = w
        part = dot(value_of(b), w, 0, 0)
        att = part if att is None else att + part
        put_value(b, dot(w, g, 1, 0))
    att = att.astype(jnp.bfloat16).astype(jnp.float32)
    row_dot = jnp.sum(att * g.astype(jnp.float32).T, axis=0, keepdims=True)
    dq = None
    for b in range(blocks):
        dw = dot(value_of(b), g, 1, 1)
        ds = (w_scr[b].astype(jnp.float32) * (dw - row_dot)).astype(jnp.bfloat16)
        part = dot(key_of(b), ds, 0, 0)
        dq = part if dq is None else dq + part
        put_key(b, dot(ds, q, 1, 0) * SCALE)
    return att.T.astype(jnp.bfloat16), (dq * SCALE).T.astype(jnp.bfloat16)


def attend_kernel(routes, *refs):
    bias_ref, q_ref, g_ref = refs[:3]
    k_refs, v_refs = refs[3 : 3 + routes], refs[3 + routes : 3 + 2 * routes]
    outs = refs[3 + 2 * routes :]
    att_ref, dq_ref = outs[:2]
    dk_refs, dv_refs = outs[2 : 2 + routes], outs[2 + routes : 2 + 2 * routes]
    s_scr, w_scr = outs[2 + 2 * routes :]

    def rows(b):
        return slice((b % TT) * TILE, (b % TT + 1) * TILE)

    def put(refs_of):
        def store(b, value):
            refs_of[b // TT][rows(b), :] = value.astype(refs_of[b // TT].dtype)

        return store

    att_ref[...], dq_ref[...] = one_head(
        q_ref[...],
        g_ref[...],
        lambda b: k_refs[b // TT][rows(b), :],
        lambda b: v_refs[b // TT][rows(b), :],
        bias_ref,
        routes * TT,
        s_scr,
        w_scr,
        put(dk_refs),
        put(dv_refs),
    )


def attend(bias, query, grad, keys, values):
    routes = len(keys)
    slab, width = query.shape
    block = pl.BlockSpec((slab, HEAD_DIM), lambda h: (0, h))
    sums = [jax.ShapeDtypeStruct((slab, width), jnp.float32 if r == 0 else jnp.bfloat16) for r in range(routes)]
    like = jax.ShapeDtypeStruct((slab, width), jnp.bfloat16)
    outs = pl.pallas_call(
        functools.partial(attend_kernel, routes),
        grid=(width // HEAD_DIM,),
        in_specs=[pl.BlockSpec(bias.shape, lambda h: (0, 0))] + [block] * (2 + 2 * routes),
        out_specs=[block] * (2 + 2 * routes),
        out_shape=[like, like] + sums + sums,
        scratch_shapes=[
            pltpu.VMEM((routes * TT, TILE, slab), jnp.float32),
            pltpu.VMEM((routes * TT, TILE, slab), jnp.bfloat16),
        ],
        compiler_params=pltpu.CompilerParams(vmem_limit_bytes=48 * 2**20),
        name="attend",
    )(bias, query, grad, *keys, *values)
    return outs[0], outs[1], outs[2 : 2 + routes], outs[2 + routes :]


def routes_of(col_count):
    seq = col_count * TH
    moves = [[(s, s ^ 1) for s in range(seq)]]
    if col_count == 2:
        moves.append([(s, s ^ TH) for s in range(seq)])
    else:
        moves.append([(s, s + TH) for s in range(seq - TH)])
        moves.append([(s, s - TH) for s in range(TH, seq)])

    def steps(row_tile, col_tile):
        found = [(0, 0, True), (1 - 2 * row_tile, 0, True)]
        if col_count == 2:
            found.append((0, 1 - 2 * col_tile, True))
        else:
            found += [(0, -1, col_tile > 0), (0, 1, col_tile < col_count - 1)]
        return found

    return moves, steps


MESH = pl.DeviceIdType.MESH


def whole_kernel(groups, seq, head, *refs):
    offsets, k_in, v_in, q_in, g_in, w_in = refs[:6]
    proj_ref, dq_ref, dk_ref, dv_ref = refs[6:10]
    mine, near, d_self, d_out, d_in, att, weight, p_out, p_in, p_self, s_scr, w_scr, bias_ref = refs[10:23]
    (x_send, x_recv, x_own, n_send, n_recv, d_send, d_recv, z_send, z_recv, y_send, y_recv, w_own, p_send, p_recv) = refs[23:]
    inputs = (k_in, v_in, q_in, g_in)
    heads, slab = mine.shape[1], mine.shape[2]
    rows = k_in.shape[0]
    half = weight.shape[2]
    width = heads * HEAD_DIM
    me_g, me_s, me_h = lax.axis_index("groups"), lax.axis_index("seq"), lax.axis_index("head")
    beside = (me_s + 1 - 2 * lax.rem(me_s, TH), lax.rem(me_s + TH, seq))

    def at(g=None, s=None, h=None):
        return (me_g if g is None else g, me_s if s is None else s, me_h if h is None else h)

    def after(i):
        return lax.rem(me_h + i, head)

    def before(i):
        return lax.rem(me_h + head - i, head)

    def remote(src, dst, send, recv, device):
        return pltpu.make_async_remote_copy(
            src_ref=src, dst_ref=dst, send_sem=send, recv_sem=recv, device_id=device, device_id_type=MESH
        )

    def columns(owner, h):
        return pl.ds(pl.multiple_of(owner * width + h * HEAD_DIM, HEAD_DIM), HEAD_DIM)

    def row_block(owner):
        return pl.ds(pl.multiple_of(owner * rows, rows), rows)

    def head_move(a, h, i, owner):
        return remote(
            inputs[a].at[:, columns(after(i), h)],
            mine.at[a, h, row_block(owner), :],
            x_send.at[a, h, i - 1],
            x_recv.at[a, h, i - 1],
            at(h=after(i)),
        )

    def head_own(a, h):
        return pltpu.make_async_copy(
            inputs[a].at[:, columns(me_h, h)], mine.at[a, h, row_block(me_h), :], x_own.at[a, h]
        )

    def near_move(j, a, h):
        return remote(mine.at[a, h], near.at[j, a, h], n_send.at[j, a, h], n_recv.at[j, a, h], at(s=beside[j]))

    def grad_move(j, a, h):
        return remote(d_out.at[j, a, h], d_in.at[j, a, h], d_send.at[j, a, h], d_recv.at[j, a, h], at(s=beside[j]))

    def weight_z(i, owner):
        return remote(
            w_in.at[pl.ds(pl.multiple_of(me_g * half, half), half), :],
            weight.at[owner, me_g],
            z_send.at[i - 1],
            z_recv.at[i - 1],
            at(s=lax.rem(me_s + i, seq)),
        )

    def weight_y(i, part):
        owner = lax.rem(me_s + seq - i, seq)
        return remote(
            weight.at[owner, me_g], weight.at[owner, part], y_send.at[i - 1], y_recv.at[i - 1], at(g=1 - me_g)
        )

    def weight_own(part):
        return pltpu.make_async_copy(
            w_in.at[pl.ds(part * half, half), :], weight.at[me_s, part], w_own.at[part]
        )

    def term_move(i):
        return remote(p_out.at[i - 1], p_in.at[i - 1], p_send.at[i - 1], p_recv.at[i - 1], at(h=after(i)))

    barrier = pltpu.get_barrier_semaphore()
    peers = [at(h=after(i)) for i in range(1, head)]
    peers += [at(s=lax.rem(me_s + i, seq)) for i in range(1, seq)] + [at(g=1 - me_g)]
    for peer in peers:
        pl.semaphore_signal(barrier, inc=1, device_id=peer, device_id_type=MESH)
    pl.semaphore_wait(barrier, len(peers))

    def send_inputs(pair):
        def step(h, carry):
            for i in range(1, head):
                for a in pair:
                    head_move(a, h, i, me_h).start()
            for a in pair:
                head_own(a, h).start()
            return carry

        lax.fori_loop(0, heads, step, 0)

    def take_inputs(a, h):
        for i in range(1, head):
            head_move(a, h, i, before(i)).wait_recv()
        head_own(a, h).wait()

    for i in range(1, seq):
        weight_z(i, me_s).start()
    send_inputs((0, 1))
    send_inputs((2, 3))
    for part in range(2):
        weight_own(part).start()

    def pass_on(h, carry):
        for a in range(2):
            take_inputs(a, h)
            for j in (1, 0):
                near_move(j, a, h).start()
        return carry

    lax.fori_loop(0, heads, pass_on, 0)

    step_r, step_c = 1 - 2 * lax.rem(me_s, TH), 1 - 2 * (me_s // TH)
    for c in range(TT):
        slots = [[offsets[c, w, x] for x in range(3)] for w in range(offsets.shape[1])]
        for r, (want_r, want_c) in enumerate(((0, 0), (step_r, 0), (0, step_c))):
            for t in range(TT):
                found = None
                for o_t, o_r, o_c in slots:
                    hit = (o_t == t - c) & (o_r == want_r) & (o_c == want_c)
                    found = hit if found is None else found | hit
                level = jnp.where(found, 0.0, DEAD).astype(jnp.float32)
                bias_ref[r * TT + t : r * TT + t + 1, c * TILE : (c + 1) * TILE] = jnp.full((1, TILE), level)

    def work(h, carry):
        take_inputs(2, h)
        take_inputs(3, h)
        for j in range(2):
            for a in range(2):
                near_move(j, a, h).wait_recv()

        def tile(b):
            return slice((b % TT) * TILE, (b % TT + 1) * TILE)

        def read(a):
            def of(b):
                r = b // TT
                return mine[a, h, tile(b), :] if r == 0 else near[r - 1, a, h, tile(b), :]

            return of

        def put(a):
            def store(b, value):
                r = b // TT
                if r == 0:
                    d_self[a, h, tile(b), :] = value
                else:
                    d_out[r - 1, a, h, tile(b), :] = value.astype(jnp.bfloat16)

            return store

        attended, dq = one_head(
            mine[2, h], mine[3, h], read(0), read(1), bias_ref, 3 * TT, s_scr, w_scr, put(0), put(1)
        )
        att[:, columns(0, h)] = attended
        dq_ref[:, columns(0, h)] = dq
        for a in range(2):
            for j in (1, 0):
                grad_move(j, a, h).start()

        @pl.when(h == heads // 2 - 1)
        def _():
            for i in range(1, seq):
                weight_z(i, lax.rem(me_s + seq - i, seq)).wait_recv()
                weight_y(i, me_g).start()

        return carry

    lax.fori_loop(0, heads, work, 0)

    for part in range(2):
        weight_own(part).wait()
    for i in range(1, seq):
        weight_y(i, 1 - me_g).wait_recv()

    def project(owner, store):
        lines = att[row_block(owner), :]
        for s in range(seq):
            for part in range(2):
                start = (s * 2 + part) * half
                store(slice(start, start + half), dot(lines, weight[s, part], 1, 1))

    for i in range(1, head):

        def to_send(cols, value, i=i):
            p_out[i - 1, :, cols] = value.astype(jnp.bfloat16)

        project(after(i), to_send)
        term_move(i).start()

    def to_keep(cols, value):
        p_self[:, cols] = value

    project(me_h, to_keep)

    def settle(h, carry):
        for a, out in ((1, dv_ref), (0, dk_ref)):
            total = d_self[a, h]
            for j in range(2):
                grad_move(j, a, h).wait_recv()
                total = total + d_in[j, a, h].astype(jnp.float32)
            out[:, columns(0, h)] = total.astype(jnp.bfloat16)
        return carry

    lax.fori_loop(0, heads, settle, 0)
    for i in range(1, head):
        term_move(i).wait_recv()
    total = p_self[...]
    for i in range(1, head):
        total = total + p_in[i - 1].astype(jnp.float32)
    proj_ref[...] = total.astype(jnp.bfloat16)

    def drain(h, carry):
        for a in range(4):
            for i in range(1, head):
                head_move(a, h, i, me_h).wait_send()
        for a in range(2):
            for j in range(2):
                near_move(j, a, h).wait_send()
                grad_move(j, a, h).wait_send()
        return carry

    lax.fori_loop(0, heads, drain, 0)
    for i in range(1, seq):
        weight_z(i, me_s).wait_send()
        weight_y(i, me_g).wait_send()
    for i in range(1, head):
        term_move(i).wait_send()


def whole(tile_offsets, key_rows, value_rows, query_rows, grad_rows, out_weight):
    groups, seq, head = (lax.axis_size(name) for name in ("groups", "seq", "head"))
    rows, features = key_rows.shape
    slab, width = rows * head, features // head
    heads = width // HEAD_DIM
    half = out_weight.shape[0] // 2
    b16, f32, dma = jnp.bfloat16, jnp.float32, pltpu.SemaphoreType.DMA
    vmem = pl.BlockSpec(memory_space=pltpu.VMEM)
    grads = jax.ShapeDtypeStruct((slab, width), b16)
    return pl.pallas_call(
        functools.partial(whole_kernel, groups, seq, head),
        in_specs=[pl.BlockSpec(memory_space=pltpu.SMEM)] + [pl.BlockSpec(memory_space=pl.ANY)] * 5,
        out_specs=[vmem] * 4,
        out_shape=[jax.ShapeDtypeStruct((rows, features), b16), grads, grads, grads],
        scratch_shapes=[
            pltpu.VMEM((4, heads, slab, HEAD_DIM), b16),
            pltpu.VMEM((2, 2, heads, slab, HEAD_DIM), b16),
            pltpu.VMEM((2, heads, slab, HEAD_DIM), f32),
            pltpu.VMEM((2, 2, heads, slab, HEAD_DIM), b16),
            pltpu.VMEM((2, 2, heads, slab, HEAD_DIM), b16),
            pltpu.VMEM((slab, width), b16),
            pltpu.VMEM((seq, 2, half, width), b16),
            pltpu.VMEM((head - 1, rows, features), b16),
            pltpu.VMEM((head - 1, rows, features), b16),
            pltpu.VMEM((rows, features), f32),
            pltpu.VMEM((3 * TT, TILE, slab), f32),
            pltpu.VMEM((3 * TT, TILE, slab), b16),
            pltpu.VMEM((3 * TT, slab), f32),
            dma((4, heads, head - 1)),
            dma((4, heads, head - 1)),
            dma((4, heads)),
            dma((2, 2, heads)),
            dma((2, 2, heads)),
            dma((2, 2, heads)),
            dma((2, 2, heads)),
            dma((seq - 1,)),
            dma((seq - 1,)),
            dma((seq - 1,)),
            dma((seq - 1,)),
            dma((2,)),
            dma((head - 1,)),
            dma((head - 1,)),
        ],
        compiler_params=pltpu.CompilerParams(
            collective_id=0, has_side_effects=True, vmem_limit_bytes=56 * 2**20
        ),
        name="whole",
    )(tile_offsets, key_rows, value_rows, query_rows, grad_rows, out_weight)


def body(query_rows, key_rows, value_rows, grad_rows, tile_offsets, out_weight):
    seq = lax.axis_size("seq")
    moves, steps = routes_of(seq // TH)
    if seq == 2 * TH and lax.axis_size("groups") == 2:
        return tuple(whole(tile_offsets, key_rows, value_rows, query_rows, grad_rows, out_weight))
    bias = live_bias(tile_offsets, lax.axis_index("seq"), steps)
    weight = lax.all_gather(out_weight, "seq", axis=0, tiled=True)
    key_h, value_h, query_h, grad_h = (
        lax.all_to_all(rows, "head", split_axis=1, concat_axis=0, tiled=True)
        for rows in (key_rows, value_rows, query_rows, grad_rows)
    )
    keys = [key_h] + [lax.ppermute(key_h, "seq", move) for move in moves]
    values = [value_h] + [lax.ppermute(value_h, "seq", move) for move in moves]
    att, dq, dk, dv = attend(bias, query_h, grad_h, keys, values)
    projected = lax.psum_scatter(
        dot(att, weight, 1, 1).astype(jnp.bfloat16), "head", scatter_dimension=0, tiled=True
    )

    def settle(terms):
        total = terms[0]
        for term, move in zip(terms[1:], moves):
            back = [(t, s) for s, t in move]
            total = total + lax.ppermute(term, "seq", back).astype(jnp.float32)
        return total.astype(jnp.bfloat16)

    return projected, dq, settle(dk), settle(dv)


def solution(mesh):
    return jax.shard_map(
        body,
        mesh=mesh,
        in_specs=(
            P(("groups", "seq", "head"), None),
            P(("groups", "seq", "head"), None),
            P(("groups", "seq", "head"), None),
            P(("groups", "seq", "head"), None),
            P("seq", None, None),
            P("seq", "head"),
        ),
        out_specs=(
            P(("groups", "seq", "head"), None),
            P(("groups", "seq"), "head"),
            P(("groups", "seq"), "head"),
            P(("groups", "seq"), "head"),
        ),
        check_vma=False,
    )
```

```python
import functools

import jax
import jax.numpy as jnp
from jax import lax
from jax.experimental import pallas as pl
from jax.experimental.pallas import tpu as pltpu
from jax.sharding import PartitionSpec as P

HEADS = 16
HEAD_DIM = 128
TILE = 256
TT = 2
TH = 2
SCALE = HEAD_DIM ** (-0.5)
DEAD = -1e30


def dot(a, b, ca, cb):
    return lax.dot_general(a, b, (((ca,), (cb,)), ((), ())), preferred_element_type=jnp.float32)


def live_bias(tile_offsets, position, steps):
    row_tile, col_tile = position % TH, position // TH
    query_time = jnp.arange(TT, dtype=jnp.int32)
    rows = []
    for step_r, step_c, there in steps(row_tile, col_tile):
        for key_time in range(TT):
            hit = (
                (tile_offsets[:, :, 0] == key_time - query_time[:, None])
                & (tile_offsets[:, :, 1] == step_r)
                & (tile_offsets[:, :, 2] == step_c)
            )
            rows.append(jnp.any(hit, axis=1) & there)
    live = jnp.stack(rows)
    return jnp.repeat(jnp.where(live, 0.0, DEAD).astype(jnp.float32), TILE, axis=1)


def one_head(q, g, key_of, value_of, bias_ref, blocks, s_scr, w_scr, put_key, put_value):
    top = None
    for b in range(blocks):
        s = dot(key_of(b), q, 1, 1) * SCALE + bias_ref[b : b + 1, :]
        s_scr[b] = s
        high = jnp.max(s, axis=0, keepdims=True)
        top = high if top is None else jnp.maximum(top, high)
    total = None
    for b in range(blocks):
        p = jnp.exp(s_scr[b] - top)
        s_scr[b] = p
        part = jnp.sum(p, axis=0, keepdims=True)
        total = part if total is None else total + part
    share = 1.0 / total
    att = None
    for b in range(blocks):
        w = (s_scr[b] * share).astype(jnp.bfloat16)
        w_scr[b] = w
        part = dot(value_of(b), w, 0, 0)
        att = part if att is None else att + part
        put_value(b, dot(w, g, 1, 0))
    att = att.astype(jnp.bfloat16).astype(jnp.float32)
    row_dot = jnp.sum(att * g.astype(jnp.float32).T, axis=0, keepdims=True)
    dq = None
    for b in range(blocks):
        dw = dot(value_of(b), g, 1, 1)
        ds = (w_scr[b].astype(jnp.float32) * (dw - row_dot)).astype(jnp.bfloat16)
        part = dot(key_of(b), ds, 0, 0)
        dq = part if dq is None else dq + part
        put_key(b, dot(ds, q, 1, 0) * SCALE)
    return att.T.astype(jnp.bfloat16), (dq * SCALE).T.astype(jnp.bfloat16)


def attend_kernel(routes, *refs):
    bias_ref, q_ref, g_ref = refs[:3]
    k_refs, v_refs = refs[3 : 3 + routes], refs[3 + routes : 3 + 2 * routes]
    outs = refs[3 + 2 * routes :]
    att_ref, dq_ref = outs[:2]
    dk_refs, dv_refs = outs[2 : 2 + routes], outs[2 + routes : 2 + 2 * routes]
    s_scr, w_scr = outs[2 + 2 * routes :]

    def rows(b):
        return slice((b % TT) * TILE, (b % TT + 1) * TILE)

    def put(refs_of):
        def store(b, value):
            refs_of[b // TT][rows(b), :] = value.astype(refs_of[b // TT].dtype)

        return store

    att_ref[...], dq_ref[...] = one_head(
        q_ref[...],
        g_ref[...],
        lambda b: k_refs[b // TT][rows(b), :],
        lambda b: v_refs[b // TT][rows(b), :],
        bias_ref,
        routes * TT,
        s_scr,
        w_scr,
        put(dk_refs),
        put(dv_refs),
    )


def attend(bias, query, grad, keys, values):
    routes = len(keys)
    slab, width = query.shape
    block = pl.BlockSpec((slab, HEAD_DIM), lambda h: (0, h))
    sums = [jax.ShapeDtypeStruct((slab, width), jnp.float32 if r == 0 else jnp.bfloat16) for r in range(routes)]
    like = jax.ShapeDtypeStruct((slab, width), jnp.bfloat16)
    outs = pl.pallas_call(
        functools.partial(attend_kernel, routes),
        grid=(width // HEAD_DIM,),
        in_specs=[pl.BlockSpec(bias.shape, lambda h: (0, 0))] + [block] * (2 + 2 * routes),
        out_specs=[block] * (2 + 2 * routes),
        out_shape=[like, like] + sums + sums,
        scratch_shapes=[
            pltpu.VMEM((routes * TT, TILE, slab), jnp.float32),
            pltpu.VMEM((routes * TT, TILE, slab), jnp.bfloat16),
        ],
        compiler_params=pltpu.CompilerParams(vmem_limit_bytes=48 * 2**20),
        name="attend",
    )(bias, query, grad, *keys, *values)
    return outs[0], outs[1], outs[2 : 2 + routes], outs[2 + routes :]


def routes_of(col_count):
    seq = col_count * TH
    moves = [[(s, s ^ 1) for s in range(seq)]]
    if col_count == 2:
        moves.append([(s, s ^ TH) for s in range(seq)])
    else:
        moves.append([(s, s + TH) for s in range(seq - TH)])
        moves.append([(s, s - TH) for s in range(TH, seq)])

    def steps(row_tile, col_tile):
        found = [(0, 0, True), (1 - 2 * row_tile, 0, True)]
        if col_count == 2:
            found.append((0, 1 - 2 * col_tile, True))
        else:
            found += [(0, -1, col_tile > 0), (0, 1, col_tile < col_count - 1)]
        return found

    return moves, steps


MESH = pl.DeviceIdType.MESH


def whole_kernel(groups, seq, head, *refs):
    offsets, k_in, v_in, q_in, g_in, w_in = refs[:6]
    proj_ref, dq_ref, dk_ref, dv_ref = refs[6:10]
    mine, near, d_self, d_out, d_in, att, weight, p_out, p_in, p_self, s_scr, w_scr, bias_ref = refs[10:23]
    (x_send, x_recv, x_own, n_send, n_recv, d_send, d_recv, z_send, z_recv, y_send, y_recv, w_own, p_send, p_recv) = refs[23:]
    inputs = (k_in, v_in, q_in, g_in)
    heads, slab = mine.shape[1], mine.shape[2]
    rows = k_in.shape[0]
    half = weight.shape[2]
    width = heads * HEAD_DIM
    me_g, me_s, me_h = lax.axis_index("groups"), lax.axis_index("seq"), lax.axis_index("head")
    beside = (me_s + 1 - 2 * lax.rem(me_s, TH), lax.rem(me_s + TH, seq))

    def at(g=None, s=None, h=None):
        return (me_g if g is None else g, me_s if s is None else s, me_h if h is None else h)

    def after(i):
        return lax.rem(me_h + i, head)

    def before(i):
        return lax.rem(me_h + head - i, head)

    def remote(src, dst, send, recv, device):
        return pltpu.make_async_remote_copy(
            src_ref=src, dst_ref=dst, send_sem=send, recv_sem=recv, device_id=device, device_id_type=MESH
        )

    def columns(owner, h):
        return pl.ds(pl.multiple_of(owner * width + h * HEAD_DIM, HEAD_DIM), HEAD_DIM)

    def row_block(owner):
        return pl.ds(pl.multiple_of(owner * rows, rows), rows)

    def head_move(a, h, i, owner):
        return remote(
            inputs[a].at[:, columns(after(i), h)],
            mine.at[a, h, row_block(owner), :],
            x_send.at[a, h, i - 1],
            x_recv.at[a, h, i - 1],
            at(h=after(i)),
        )

    def head_own(a, h):
        return pltpu.make_async_copy(
            inputs[a].at[:, columns(me_h, h)], mine.at[a, h, row_block(me_h), :], x_own.at[a, h]
        )

    def near_move(j, h):
        return remote(mine.at[0:2, h], near.at[j, :, h], n_send.at[j, h], n_recv.at[j, h], at(s=beside[j]))

    def grad_move(j, h):
        return remote(d_out.at[j, :, h], d_in.at[j, :, h], d_send.at[j, h], d_recv.at[j, h], at(s=beside[j]))

    def weight_z(i, owner):
        return remote(
            w_in.at[pl.ds(pl.multiple_of(me_g * half, half), half), :],
            weight.at[owner, me_g],
            z_send.at[i - 1],
            z_recv.at[i - 1],
            at(s=lax.rem(me_s + i, seq)),
        )

    def weight_y(i, part):
        owner = lax.rem(me_s + seq - i, seq)
        return remote(
            weight.at[owner, me_g], weight.at[owner, part], y_send.at[i - 1], y_recv.at[i - 1], at(g=1 - me_g)
        )

    def weight_own(part):
        return pltpu.make_async_copy(
            w_in.at[pl.ds(part * half, half), :], weight.at[me_s, part], w_own.at[part]
        )

    def term_move(i):
        return remote(p_out.at[i - 1], p_in.at[i - 1], p_send.at[i - 1], p_recv.at[i - 1], at(h=after(i)))

    barrier = pltpu.get_barrier_semaphore()
    peers = [at(h=after(i)) for i in range(1, head)]
    peers += [at(s=lax.rem(me_s + i, seq)) for i in range(1, seq)] + [at(g=1 - me_g)]
    for peer in peers:
        pl.semaphore_signal(barrier, inc=1, device_id=peer, device_id_type=MESH)
    pl.semaphore_wait(barrier, len(peers))

    def send_inputs(pair):
        def step(h, carry):
            for i in range(1, head):
                for a in pair:
                    head_move(a, h, i, me_h).start()
            for a in pair:
                head_own(a, h).start()
            return carry

        lax.fori_loop(0, heads, step, 0)

    def take_inputs(a, h):
        for i in range(1, head):
            head_move(a, h, i, before(i)).wait_recv()
        head_own(a, h).wait()

    for i in range(1, seq):
        weight_z(i, me_s).start()
    send_inputs((0, 1))
    send_inputs((2, 3))
    for part in range(2):
        weight_own(part).start()

    def pass_on(h, carry):
        for a in range(2):
            take_inputs(a, h)
        for j in (1, 0):
            near_move(j, h).start()
        return carry

    lax.fori_loop(0, heads, pass_on, 0)

    step_r, step_c = 1 - 2 * lax.rem(me_s, TH), 1 - 2 * (me_s // TH)
    for c in range(TT):
        slots = [[offsets[c, w, x] for x in range(3)] for w in range(offsets.shape[1])]
        for r, (want_r, want_c) in enumerate(((0, 0), (step_r, 0), (0, step_c))):
            for t in range(TT):
                found = None
                for o_t, o_r, o_c in slots:
                    hit = (o_t == t - c) & (o_r == want_r) & (o_c == want_c)
                    found = hit if found is None else found | hit
                level = jnp.where(found, 0.0, DEAD).astype(jnp.float32)
                bias_ref[r * TT + t : r * TT + t + 1, c * TILE : (c + 1) * TILE] = jnp.full((1, TILE), level)

    def work(h, carry):
        take_inputs(2, h)
        take_inputs(3, h)
        for j in range(2):
            near_move(j, h).wait_recv()

        def tile(b):
            return slice((b % TT) * TILE, (b % TT + 1) * TILE)

        def read(a):
            def of(b):
                r = b // TT
                return mine[a, h, tile(b), :] if r == 0 else near[r - 1, a, h, tile(b), :]

            return of

        def put(a):
            def store(b, value):
                r = b // TT
                if r == 0:
                    d_self[a, h, tile(b), :] = value
                else:
                    d_out[r - 1, a, h, tile(b), :] = value.astype(jnp.bfloat16)

            return store

        attended, dq = one_head(
            mine[2, h], mine[3, h], read(0), read(1), bias_ref, 3 * TT, s_scr, w_scr, put(0), put(1)
        )
        att[:, columns(0, h)] = attended
        dq_ref[:, columns(0, h)] = dq
        for j in (1, 0):
            grad_move(j, h).start()

        @pl.when(h == heads // 2 - 1)
        def _():
            for i in range(1, seq):
                weight_z(i, lax.rem(me_s + seq - i, seq)).wait_recv()
                weight_y(i, me_g).start()

        return carry

    lax.fori_loop(0, heads, work, 0)

    for part in range(2):
        weight_own(part).wait()
    for i in range(1, seq):
        weight_y(i, 1 - me_g).wait_recv()

    def project(owner, store):
        lines = att[row_block(owner), :]
        for s in range(seq):
            for part in range(2):
                start = (s * 2 + part) * half
                store(slice(start, start + half), dot(lines, weight[s, part], 1, 1))

    for i in range(1, head):

        def to_send(cols, value, i=i):
            p_out[i - 1, :, cols] = value.astype(jnp.bfloat16)

        project(after(i), to_send)
        term_move(i).start()

    def to_keep(cols, value):
        p_self[:, cols] = value

    project(me_h, to_keep)

    def settle(h, carry):
        for j in range(2):
            grad_move(j, h).wait_recv()
        for a, out in ((1, dv_ref), (0, dk_ref)):
            total = d_self[a, h]
            for j in range(2):
                total = total + d_in[j, a, h].astype(jnp.float32)
            out[:, columns(0, h)] = total.astype(jnp.bfloat16)
        return carry

    lax.fori_loop(0, heads, settle, 0)
    for i in range(1, head):
        term_move(i).wait_recv()
    total = p_self[...]
    for i in range(1, head):
        total = total + p_in[i - 1].astype(jnp.float32)
    proj_ref[...] = total.astype(jnp.bfloat16)

    def drain(h, carry):
        for a in range(4):
            for i in range(1, head):
                head_move(a, h, i, me_h).wait_send()
        for j in range(2):
            near_move(j, h).wait_send()
            grad_move(j, h).wait_send()
        return carry

    lax.fori_loop(0, heads, drain, 0)
    for i in range(1, seq):
        weight_z(i, me_s).wait_send()
        weight_y(i, me_g).wait_send()
    for i in range(1, head):
        term_move(i).wait_send()


def whole(tile_offsets, key_rows, value_rows, query_rows, grad_rows, out_weight):
    groups, seq, head = (lax.axis_size(name) for name in ("groups", "seq", "head"))
    rows, features = key_rows.shape
    slab, width = rows * head, features // head
    heads = width // HEAD_DIM
    half = out_weight.shape[0] // 2
    b16, f32, dma = jnp.bfloat16, jnp.float32, pltpu.SemaphoreType.DMA
    vmem = pl.BlockSpec(memory_space=pltpu.VMEM)
    grads = jax.ShapeDtypeStruct((slab, width), b16)
    return pl.pallas_call(
        functools.partial(whole_kernel, groups, seq, head),
        in_specs=[pl.BlockSpec(memory_space=pltpu.SMEM)] + [pl.BlockSpec(memory_space=pl.ANY)] * 5,
        out_specs=[vmem] * 4,
        out_shape=[jax.ShapeDtypeStruct((rows, features), b16), grads, grads, grads],
        scratch_shapes=[
            pltpu.VMEM((4, heads, slab, HEAD_DIM), b16),
            pltpu.VMEM((2, 2, heads, slab, HEAD_DIM), b16),
            pltpu.VMEM((2, heads, slab, HEAD_DIM), f32),
            pltpu.VMEM((2, 2, heads, slab, HEAD_DIM), b16),
            pltpu.VMEM((2, 2, heads, slab, HEAD_DIM), b16),
            pltpu.VMEM((slab, width), b16),
            pltpu.VMEM((seq, 2, half, width), b16),
            pltpu.VMEM((head - 1, rows, features), b16),
            pltpu.VMEM((head - 1, rows, features), b16),
            pltpu.VMEM((rows, features), f32),
            pltpu.VMEM((3 * TT, TILE, slab), f32),
            pltpu.VMEM((3 * TT, TILE, slab), b16),
            pltpu.VMEM((3 * TT, slab), f32),
            dma((4, heads, head - 1)),
            dma((4, heads, head - 1)),
            dma((4, heads)),
            dma((2, heads)),
            dma((2, heads)),
            dma((2, heads)),
            dma((2, heads)),
            dma((seq - 1,)),
            dma((seq - 1,)),
            dma((seq - 1,)),
            dma((seq - 1,)),
            dma((2,)),
            dma((head - 1,)),
            dma((head - 1,)),
        ],
        compiler_params=pltpu.CompilerParams(
            collective_id=0, has_side_effects=True, vmem_limit_bytes=56 * 2**20
        ),
        name="whole",
    )(tile_offsets, key_rows, value_rows, query_rows, grad_rows, out_weight)


def body(query_rows, key_rows, value_rows, grad_rows, tile_offsets, out_weight):
    seq = lax.axis_size("seq")
    moves, steps = routes_of(seq // TH)
    if seq == 2 * TH and lax.axis_size("groups") == 2:
        return tuple(whole(tile_offsets, key_rows, value_rows, query_rows, grad_rows, out_weight))
    bias = live_bias(tile_offsets, lax.axis_index("seq"), steps)
    weight = lax.all_gather(out_weight, "seq", axis=0, tiled=True)
    key_h, value_h, query_h, grad_h = (
        lax.all_to_all(rows, "head", split_axis=1, concat_axis=0, tiled=True)
        for rows in (key_rows, value_rows, query_rows, grad_rows)
    )
    keys = [key_h] + [lax.ppermute(key_h, "seq", move) for move in moves]
    values = [value_h] + [lax.ppermute(value_h, "seq", move) for move in moves]
    att, dq, dk, dv = attend(bias, query_h, grad_h, keys, values)
    projected = lax.psum_scatter(
        dot(att, weight, 1, 1).astype(jnp.bfloat16), "head", scatter_dimension=0, tiled=True
    )

    def settle(terms):
        total = terms[0]
        for term, move in zip(terms[1:], moves):
            back = [(t, s) for s, t in move]
            total = total + lax.ppermute(term, "seq", back).astype(jnp.float32)
        return total.astype(jnp.bfloat16)

    return projected, dq, settle(dk), settle(dv)


def solution(mesh):
    return jax.shard_map(
        body,
        mesh=mesh,
        in_specs=(
            P(("groups", "seq", "head"), None),
            P(("groups", "seq", "head"), None),
            P(("groups", "seq", "head"), None),
            P(("groups", "seq", "head"), None),
            P("seq", None, None),
            P("seq", "head"),
        ),
        out_specs=(
            P(("groups", "seq", "head"), None),
            P(("groups", "seq"), "head"),
            P(("groups", "seq"), "head"),
            P(("groups", "seq"), "head"),
        ),
        check_vma=False,
    )
```

```python
import functools

import jax
import jax.numpy as jnp
from jax import lax
from jax.experimental import pallas as pl
from jax.experimental.pallas import tpu as pltpu
from jax.sharding import PartitionSpec as P

HEADS = 16
HEAD_DIM = 128
TILE = 256
TT = 2
TH = 2
SCALE = HEAD_DIM ** (-0.5)
DEAD = -1e30


def dot(a, b, ca, cb):
    return lax.dot_general(a, b, (((ca,), (cb,)), ((), ())), preferred_element_type=jnp.float32)


def live_bias(tile_offsets, position, steps):
    row_tile, col_tile = position % TH, position // TH
    query_time = jnp.arange(TT, dtype=jnp.int32)
    rows = []
    for step_r, step_c, there in steps(row_tile, col_tile):
        for key_time in range(TT):
            hit = (
                (tile_offsets[:, :, 0] == key_time - query_time[:, None])
                & (tile_offsets[:, :, 1] == step_r)
                & (tile_offsets[:, :, 2] == step_c)
            )
            rows.append(jnp.any(hit, axis=1) & there)
    live = jnp.stack(rows)
    return jnp.repeat(jnp.where(live, 0.0, DEAD).astype(jnp.float32), TILE, axis=1)


def one_head(q, g, key_of, value_of, bias_ref, blocks, s_scr, w_scr, put_key, put_value):
    top = None
    for b in range(blocks):
        s = dot(key_of(b), q, 1, 1) * SCALE + bias_ref[b : b + 1, :]
        s_scr[b] = s
        high = jnp.max(s, axis=0, keepdims=True)
        top = high if top is None else jnp.maximum(top, high)
    total = None
    for b in range(blocks):
        p = jnp.exp(s_scr[b] - top)
        s_scr[b] = p
        part = jnp.sum(p, axis=0, keepdims=True)
        total = part if total is None else total + part
    share = 1.0 / total
    att = None
    for b in range(blocks):
        w = (s_scr[b] * share).astype(jnp.bfloat16)
        w_scr[b] = w
        part = dot(value_of(b), w, 0, 0)
        att = part if att is None else att + part
        put_value(b, dot(w, g, 1, 0))
    att = att.astype(jnp.bfloat16).astype(jnp.float32)
    row_dot = jnp.sum(att * g.astype(jnp.float32).T, axis=0, keepdims=True)
    dq = None
    for b in range(blocks):
        dw = dot(value_of(b), g, 1, 1)
        ds = (w_scr[b].astype(jnp.float32) * (dw - row_dot)).astype(jnp.bfloat16)
        part = dot(key_of(b), ds, 0, 0)
        dq = part if dq is None else dq + part
        put_key(b, dot(ds, q, 1, 0) * SCALE)
    return att.T.astype(jnp.bfloat16), (dq * SCALE).T.astype(jnp.bfloat16)


def attend_kernel(routes, *refs):
    bias_ref, q_ref, g_ref = refs[:3]
    k_refs, v_refs = refs[3 : 3 + routes], refs[3 + routes : 3 + 2 * routes]
    outs = refs[3 + 2 * routes :]
    att_ref, dq_ref = outs[:2]
    dk_refs, dv_refs = outs[2 : 2 + routes], outs[2 + routes : 2 + 2 * routes]
    s_scr, w_scr = outs[2 + 2 * routes :]

    def rows(b):
        return slice((b % TT) * TILE, (b % TT + 1) * TILE)

    def put(refs_of):
        def store(b, value):
            refs_of[b // TT][rows(b), :] = value.astype(refs_of[b // TT].dtype)

        return store

    att_ref[...], dq_ref[...] = one_head(
        q_ref[...],
        g_ref[...],
        lambda b: k_refs[b // TT][rows(b), :],
        lambda b: v_refs[b // TT][rows(b), :],
        bias_ref,
        routes * TT,
        s_scr,
        w_scr,
        put(dk_refs),
        put(dv_refs),
    )


def attend(bias, query, grad, keys, values):
    routes = len(keys)
    slab, width = query.shape
    block = pl.BlockSpec((slab, HEAD_DIM), lambda h: (0, h))
    sums = [jax.ShapeDtypeStruct((slab, width), jnp.float32 if r == 0 else jnp.bfloat16) for r in range(routes)]
    like = jax.ShapeDtypeStruct((slab, width), jnp.bfloat16)
    outs = pl.pallas_call(
        functools.partial(attend_kernel, routes),
        grid=(width // HEAD_DIM,),
        in_specs=[pl.BlockSpec(bias.shape, lambda h: (0, 0))] + [block] * (2 + 2 * routes),
        out_specs=[block] * (2 + 2 * routes),
        out_shape=[like, like] + sums + sums,
        scratch_shapes=[
            pltpu.VMEM((routes * TT, TILE, slab), jnp.float32),
            pltpu.VMEM((routes * TT, TILE, slab), jnp.bfloat16),
        ],
        compiler_params=pltpu.CompilerParams(vmem_limit_bytes=48 * 2**20),
        name="attend",
    )(bias, query, grad, *keys, *values)
    return outs[0], outs[1], outs[2 : 2 + routes], outs[2 + routes :]


def routes_of(col_count):
    seq = col_count * TH
    moves = [[(s, s ^ 1) for s in range(seq)]]
    if col_count == 2:
        moves.append([(s, s ^ TH) for s in range(seq)])
    else:
        moves.append([(s, s + TH) for s in range(seq - TH)])
        moves.append([(s, s - TH) for s in range(TH, seq)])

    def steps(row_tile, col_tile):
        found = [(0, 0, True), (1 - 2 * row_tile, 0, True)]
        if col_count == 2:
            found.append((0, 1 - 2 * col_tile, True))
        else:
            found += [(0, -1, col_tile > 0), (0, 1, col_tile < col_count - 1)]
        return found

    return moves, steps


MESH = pl.DeviceIdType.MESH


def whole_kernel(groups, seq, head, *refs):
    offsets, k_in, v_in, q_in, g_in, w_in = refs[:6]
    proj_ref, dq_ref, dk_ref, dv_ref = refs[6:10]
    mine, near, d_self, d_out, d_in, att, weight, p_out, p_in, p_self, s_scr, w_scr, bias_ref = refs[10:23]
    (x_send, x_recv, x_own, n_send, n_recv, d_send, d_recv, z_send, z_recv, y_send, y_recv, w_own, p_send, p_recv) = refs[23:]
    inputs = (k_in, v_in, q_in, g_in)
    heads, slab = mine.shape[1], mine.shape[2]
    rows = k_in.shape[0]
    half = weight.shape[2]
    width = heads * HEAD_DIM
    me_g, me_s, me_h = lax.axis_index("groups"), lax.axis_index("seq"), lax.axis_index("head")
    beside = (me_s + 1 - 2 * lax.rem(me_s, TH), lax.rem(me_s + TH, seq))

    def at(g=None, s=None, h=None):
        return (me_g if g is None else g, me_s if s is None else s, me_h if h is None else h)

    def after(i):
        return lax.rem(me_h + i, head)

    def before(i):
        return lax.rem(me_h + head - i, head)

    def remote(src, dst, send, recv, device):
        return pltpu.make_async_remote_copy(
            src_ref=src, dst_ref=dst, send_sem=send, recv_sem=recv, device_id=device, device_id_type=MESH
        )

    def columns(owner, h):
        return pl.ds(pl.multiple_of(owner * width + h * HEAD_DIM, HEAD_DIM), HEAD_DIM)

    def row_block(owner):
        return pl.ds(pl.multiple_of(owner * rows, rows), rows)

    def head_move(a, h, i, owner):
        return remote(
            inputs[a].at[:, columns(after(i), h)],
            mine.at[a, h, row_block(owner), :],
            x_send.at[a, h, i - 1],
            x_recv.at[a, h, i - 1],
            at(h=after(i)),
        )

    def head_own(a, h):
        return pltpu.make_async_copy(
            inputs[a].at[:, columns(me_h, h)], mine.at[a, h, row_block(me_h), :], x_own.at[a, h]
        )

    def near_move(j, h):
        return remote(mine.at[0:2, h], near.at[j, :, h], n_send.at[j, h], n_recv.at[j, h], at(s=beside[j]))

    def grad_move(j, h):
        return remote(d_out.at[j, :, h], d_in.at[j, :, h], d_send.at[j, h], d_recv.at[j, h], at(s=beside[j]))

    def weight_z(i, owner):
        return remote(
            w_in.at[pl.ds(pl.multiple_of(me_g * half, half), half), :],
            weight.at[owner, me_g],
            z_send.at[i - 1],
            z_recv.at[i - 1],
            at(s=lax.rem(me_s + i, seq)),
        )

    def weight_y(i, part):
        owner = lax.rem(me_s + seq - i, seq)
        return remote(
            weight.at[owner, me_g], weight.at[owner, part], y_send.at[i - 1], y_recv.at[i - 1], at(g=1 - me_g)
        )

    def weight_own(part):
        return pltpu.make_async_copy(
            w_in.at[pl.ds(part * half, half), :], weight.at[me_s, part], w_own.at[part]
        )

    def term_move(i):
        return remote(p_out.at[i - 1], p_in.at[i - 1], p_send.at[i - 1], p_recv.at[i - 1], at(h=after(i)))

    barrier = pltpu.get_barrier_semaphore()
    peers = [at(h=after(i)) for i in range(1, head)]
    peers += [at(s=lax.rem(me_s + i, seq)) for i in range(1, seq)] + [at(g=1 - me_g)]
    for peer in peers:
        pl.semaphore_signal(barrier, inc=1, device_id=peer, device_id_type=MESH)
    pl.semaphore_wait(barrier, len(peers))

    def send_inputs(pair):
        def step(h, carry):
            for i in range(1, head):
                for a in pair:
                    head_move(a, h, i, me_h).start()
            for a in pair:
                head_own(a, h).start()
            return carry

        lax.fori_loop(0, heads, step, 0)

    def take_inputs(a, h):
        for i in range(1, head):
            head_move(a, h, i, before(i)).wait_recv()
        head_own(a, h).wait()

    for i in range(1, seq):
        weight_z(i, me_s).start()
    send_inputs((0, 1))
    send_inputs((2, 3))
    for part in range(2):
        weight_own(part).start()

    def pass_on(h, carry):
        for a in range(2):
            take_inputs(a, h)
        for j in range(2):
            near_move(j, h).start()
        return carry

    lax.fori_loop(0, heads, pass_on, 0)

    step_r, step_c = 1 - 2 * lax.rem(me_s, TH), 1 - 2 * (me_s // TH)
    for c in range(TT):
        slots = [[offsets[c, w, x] for x in range(3)] for w in range(offsets.shape[1])]
        for r, (want_r, want_c) in enumerate(((0, 0), (step_r, 0), (0, step_c))):
            for t in range(TT):
                found = None
                for o_t, o_r, o_c in slots:
                    hit = (o_t == t - c) & (o_r == want_r) & (o_c == want_c)
                    found = hit if found is None else found | hit
                level = jnp.where(found, 0.0, DEAD).astype(jnp.float32)
                bias_ref[r * TT + t : r * TT + t + 1, c * TILE : (c + 1) * TILE] = jnp.full((1, TILE), level)

    def work(h, carry):
        take_inputs(2, h)
        take_inputs(3, h)
        for j in range(2):
            near_move(j, h).wait_recv()

        def tile(b):
            return slice((b % TT) * TILE, (b % TT + 1) * TILE)

        def read(a):
            def of(b):
                r = b // TT
                return mine[a, h, tile(b), :] if r == 0 else near[r - 1, a, h, tile(b), :]

            return of

        def put(a):
            def store(b, value):
                r = b // TT
                if r == 0:
                    d_self[a, h, tile(b), :] = value
                else:
                    d_out[r - 1, a, h, tile(b), :] = value.astype(jnp.bfloat16)

            return store

        attended, dq = one_head(
            mine[2, h], mine[3, h], read(0), read(1), bias_ref, 3 * TT, s_scr, w_scr, put(0), put(1)
        )
        att[:, columns(0, h)] = attended
        dq_ref[:, columns(0, h)] = dq
        for j in range(2):
            grad_move(j, h).start()

        @pl.when(h == heads // 2 - 1)
        def _():
            for i in range(1, seq):
                weight_z(i, lax.rem(me_s + seq - i, seq)).wait_recv()
                weight_y(i, me_g).start()

        return carry

    lax.fori_loop(0, heads, work, 0)

    for part in range(2):
        weight_own(part).wait()
    for i in range(1, seq):
        weight_y(i, 1 - me_g).wait_recv()

    def project(owner, store):
        lines = att[row_block(owner), :]
        for s in range(seq):
            for part in range(2):
                start = (s * 2 + part) * half
                store(slice(start, start + half), dot(lines, weight[s, part], 1, 1))

    for i in range(1, head):

        def to_send(cols, value, i=i):
            p_out[i - 1, :, cols] = value.astype(jnp.bfloat16)

        project(after(i), to_send)
        term_move(i).start()

    def to_keep(cols, value):
        p_self[:, cols] = value

    project(me_h, to_keep)

    def settle(h, carry):
        for j in range(2):
            grad_move(j, h).wait_recv()
        for a, out in ((1, dv_ref), (0, dk_ref)):
            total = d_self[a, h]
            for j in range(2):
                total = total + d_in[j, a, h].astype(jnp.float32)
            out[:, columns(0, h)] = total.astype(jnp.bfloat16)
        return carry

    lax.fori_loop(0, heads, settle, 0)
    for i in range(1, head):
        term_move(i).wait_recv()
    total = p_self[...]
    for i in range(1, head):
        total = total + p_in[i - 1].astype(jnp.float32)
    proj_ref[...] = total.astype(jnp.bfloat16)

    def drain(h, carry):
        for a in range(4):
            for i in range(1, head):
                head_move(a, h, i, me_h).wait_send()
        for j in range(2):
            near_move(j, h).wait_send()
            grad_move(j, h).wait_send()
        return carry

    lax.fori_loop(0, heads, drain, 0)
    for i in range(1, seq):
        weight_z(i, me_s).wait_send()
        weight_y(i, me_g).wait_send()
    for i in range(1, head):
        term_move(i).wait_send()


def whole(tile_offsets, key_rows, value_rows, query_rows, grad_rows, out_weight):
    groups, seq, head = (lax.axis_size(name) for name in ("groups", "seq", "head"))
    rows, features = key_rows.shape
    slab, width = rows * head, features // head
    heads = width // HEAD_DIM
    half = out_weight.shape[0] // 2
    b16, f32, dma = jnp.bfloat16, jnp.float32, pltpu.SemaphoreType.DMA
    vmem = pl.BlockSpec(memory_space=pltpu.VMEM)
    grads = jax.ShapeDtypeStruct((slab, width), b16)
    return pl.pallas_call(
        functools.partial(whole_kernel, groups, seq, head),
        in_specs=[pl.BlockSpec(memory_space=pltpu.SMEM)] + [pl.BlockSpec(memory_space=pl.ANY)] * 5,
        out_specs=[vmem] * 4,
        out_shape=[jax.ShapeDtypeStruct((rows, features), b16), grads, grads, grads],
        scratch_shapes=[
            pltpu.VMEM((4, heads, slab, HEAD_DIM), b16),
            pltpu.VMEM((2, 2, heads, slab, HEAD_DIM), b16),
            pltpu.VMEM((2, heads, slab, HEAD_DIM), f32),
            pltpu.VMEM((2, 2, heads, slab, HEAD_DIM), b16),
            pltpu.VMEM((2, 2, heads, slab, HEAD_DIM), b16),
            pltpu.VMEM((slab, width), b16),
            pltpu.VMEM((seq, 2, half, width), b16),
            pltpu.VMEM((head - 1, rows, features), b16),
            pltpu.VMEM((head - 1, rows, features), b16),
            pltpu.VMEM((rows, features), f32),
            pltpu.VMEM((3 * TT, TILE, slab), f32),
            pltpu.VMEM((3 * TT, TILE, slab), b16),
            pltpu.VMEM((3 * TT, slab), f32),
            dma((4, heads, head - 1)),
            dma((4, heads, head - 1)),
            dma((4, heads)),
            dma((2, heads)),
            dma((2, heads)),
            dma((2, heads)),
            dma((2, heads)),
            dma((seq - 1,)),
            dma((seq - 1,)),
            dma((seq - 1,)),
            dma((seq - 1,)),
            dma((2,)),
            dma((head - 1,)),
            dma((head - 1,)),
        ],
        compiler_params=pltpu.CompilerParams(
            collective_id=0, has_side_effects=True, vmem_limit_bytes=56 * 2**20
        ),
        name="whole",
    )(tile_offsets, key_rows, value_rows, query_rows, grad_rows, out_weight)


def body(query_rows, key_rows, value_rows, grad_rows, tile_offsets, out_weight):
    seq = lax.axis_size("seq")
    moves, steps = routes_of(seq // TH)
    if seq == 2 * TH and lax.axis_size("groups") == 2:
        return tuple(whole(tile_offsets, key_rows, value_rows, query_rows, grad_rows, out_weight))
    bias = live_bias(tile_offsets, lax.axis_index("seq"), steps)
    weight = lax.all_gather(out_weight, "seq", axis=0, tiled=True)
    key_h, value_h, query_h, grad_h = (
        lax.all_to_all(rows, "head", split_axis=1, concat_axis=0, tiled=True)
        for rows in (key_rows, value_rows, query_rows, grad_rows)
    )
    keys = [key_h] + [lax.ppermute(key_h, "seq", move) for move in moves]
    values = [value_h] + [lax.ppermute(value_h, "seq", move) for move in moves]
    att, dq, dk, dv = attend(bias, query_h, grad_h, keys, values)
    projected = lax.psum_scatter(
        dot(att, weight, 1, 1).astype(jnp.bfloat16), "head", scatter_dimension=0, tiled=True
    )

    def settle(terms):
        total = terms[0]
        for term, move in zip(terms[1:], moves):
            back = [(t, s) for s, t in move]
            total = total + lax.ppermute(term, "seq", back).astype(jnp.float32)
        return total.astype(jnp.bfloat16)

    return projected, dq, settle(dk), settle(dv)


def solution(mesh):
    return jax.shard_map(
        body,
        mesh=mesh,
        in_specs=(
            P(("groups", "seq", "head"), None),
            P(("groups", "seq", "head"), None),
            P(("groups", "seq", "head"), None),
            P(("groups", "seq", "head"), None),
            P("seq", None, None),
            P("seq", "head"),
        ),
        out_specs=(
            P(("groups", "seq", "head"), None),
            P(("groups", "seq"), "head"),
            P(("groups", "seq"), "head"),
            P(("groups", "seq"), "head"),
        ),
        check_vma=False,
    )
```
